32 devices in a mesh: dom: 2 (over y), row: 16 (over z, x, core).
Axes of the slice: x: 2, y: 2, z: 4, core: 2. Of those that a mesh axis runs over, the one named last changes fastest.
Arguments:
- memory: bfloat16 [65536, 256], P(('dom', 'row')), may hold values from -5 to 5
- node_time: int32 [65536], P(('dom', 'row')), may hold values from 0 to 999
- target: int32 [4, 16384], P(None, ('dom', 'row')), may hold values from -1 to 2047
- source: int32 [4, 16384], P(None, ('dom', 'row')), may hold values from 0 to 65535, as said below
- event_time: int32 [4, 16384], P(None, ('dom', 'row')), may hold values from 1000 to 2999
- edge_feat: bfloat16 [4, 16384, 128], P(None, ('dom', 'row')), may hold values from -5 to 5
- owner_group: int32 [4], replicated, may hold values from 0 to 1
- w_message: bfloat16 [768, 256], replicated, may hold values from -0.21875 to 0.21875
- frequency: float32 [128], replicated, may hold values from 0.001 to 0.1
- phase_shift: float32 [128], replicated, may hold values from -3.140625 to 3.140625
- w_input: bfloat16 [256, 768], replicated, may hold values from -0.375 to 0.375
- w_hidden: bfloat16 [256, 768], replicated, may hold values from -0.375 to 0.375
- bias_input: float32 [768], replicated, may hold values from -3 to 3
- bias_hidden: float32 [768], replicated, may hold values from -3 to 3
Outputs:
- new_memory: bfloat16 [65536, 256], P(('dom', 'row'))
The draws below stay inside these ranges and needn't reach their ends.
Inputs may be any that keep to these rules, and one draw needn't show every extreme that they name: `target`: -1 marks a padded event row. `source`: values under 32768 name the event's own group, the rest the owner group of the batch; in each batch, of the events of one device at most 48 have a value v < 32768 with v // 2048 equal to one given r, and at most 16 have v >= 32768 with (v - 32768) // 2048 equal to one given r; on every device and batch some r reaches 48 and some r reaches 16.
All inputs are finite; a program needn't handle non-finite values.
Results may differ from the reference program's by a relative error of at most 0.0034.
Values may be sent and summed in bfloat16 or wider, within the bound.
A program may use at most 64 MiB of HBM per device.

```python
import math
import jax
import jax.numpy as jnp
from jax import lax

W = 256
MSG = 256
TD = 128
EF = 128
B = 4
NODE_DEV = 2048
EV_DEV = 512
NODES = 65536
EVENTS = 16384
N_DOM = 2
N_ROW = 16


def draw_source(key, part):
    cap = 3 * EV_DEV // (2 * N_ROW)
    ocap = EV_DEV // (2 * N_ROW)
    per = cap + ocap
    slots = N_ROW * per
    blocks = B * N_DOM * N_ROW
    first_key, own_key, far_key, node_key = jax.random.split(jax.random.fold_in(key, 17), 4)
    scores = jax.random.randint(first_key, (blocks, slots), 0, 1 << 20)
    full_own = jax.random.randint(own_key, (blocks, 1), 0, N_ROW)
    full_far = jax.random.randint(far_key, (blocks, 1), 0, N_ROW)
    slot_ids = jnp.arange(slots, dtype=jnp.int32)[None, :]
    bucket = slot_ids // per
    is_far = slot_ids % per >= cap
    forced = (bucket == full_own) & jnp.logical_not(is_far) | (bucket == full_far) & is_far
    scores = jnp.where(forced, -1, scores)
    order = jnp.argsort(scores, axis=1, stable=True)[:, :EV_DEV].astype(jnp.int32)
    chosen_bucket = order // per
    chosen_far = order % per >= cap
    node = jax.random.randint(node_key, (blocks, EV_DEV), 0, NODE_DEV)
    local = chosen_bucket * NODE_DEV + node
    value = jnp.where(chosen_far, local + N_ROW * NODE_DEV, local)
    return value.reshape(B, N_DOM * N_ROW * EV_DEV).astype(jnp.int32)


def plant(result, rng, low, high):
    extent = result.shape
    spot = [jax.random.randint(jax.random.fold_in(rng, axis), (), 0, extent[axis]) for axis in range(len(extent))]
    result = result.at[tuple(spot)].set(low)
    longest = extent.index(max(extent))
    spot[longest] = (spot[longest] + 1) % extent[longest]
    return result.at[tuple(spot)].set(high)


def steps_of(key, shape, cuts, smallest, high):
    factor_of = 1.0
    for position, blocks in cuts:
        heights = jax.random.uniform(jax.random.fold_in(jax.random.fold_in(key, 6), position), (blocks,), jnp.float32, smallest / len(cuts), high / len(cuts))
        factor_of = factor_of * jnp.repeat(jnp.exp(heights), shape[position] // blocks).reshape((-1,) + (1,) * (len(shape) - 1 - position))
    return factor_of


def normal_values(key, shape, spread, bound, cuts=(), held_as=jnp.bfloat16):
    entries = spread * jax.random.normal(key, shape, jnp.float32)
    if cuts:
        entries = entries * steps_of(key, shape, cuts, -0.22, 0.18)
    return jnp.clip(entries, -bound, bound).astype(held_as)


def setup_inputs(seed: int = 0) -> dict:
    key_list = jax.random.split(jax.random.key(seed), 15)
    memory = normal_values(key_list[0], (NODES, W), 1.0, 5.0, ((0, 32),))
    node_time = plant(jax.random.randint(key_list[1], (NODES,), 0, 1000), jax.random.fold_in(key_list[1], 1), 0, 999).astype(jnp.int32)
    target = plant(jax.random.randint(key_list[2], (B, EVENTS), -1, NODE_DEV), jax.random.fold_in(key_list[2], 1), -1, NODE_DEV - 1).astype(jnp.int32)
    source = draw_source(jax.random.fold_in(key_list[14], 71), 0)
    event_time = plant(jax.random.randint(key_list[4], (B, EVENTS), 1000, 3000), jax.random.fold_in(key_list[4], 1), 1000, 2999).astype(jnp.int32)
    edge_feat = normal_values(key_list[5], (B, EVENTS, EF), 1.0, 5.0, ((1, 32),))
    owner_group = plant(jax.random.randint(key_list[6], (B,), 0, N_DOM), jax.random.fold_in(key_list[6], 1), 0, N_DOM - 1).astype(jnp.int32)
    w_message = normal_values(key_list[7], (2 * W + TD + EF, MSG), (2 * W + TD + EF) ** -0.5, 0.21875)
    frequency = jnp.clip(jnp.exp(jax.random.uniform(key_list[8], (TD,), jnp.float32, math.log(0.001), math.log(0.1))), 0.001, 0.1)
    phase_shift = jnp.clip(jax.random.uniform(key_list[9], (TD,), jnp.float32, -3.140625, 3.140625), -3.140625, 3.140625)
    w_input = normal_values(key_list[10], (MSG, 3 * W), MSG ** -0.5, 0.375)
    w_hidden = normal_values(key_list[11], (W, 3 * W), W ** -0.5, 0.375)
    bias_input = normal_values(key_list[12], (3 * W,), 0.5, 3.0, (), jnp.float32)
    bias_hidden = normal_values(key_list[13], (3 * W,), 0.5, 3.0, (), jnp.float32)
    return dict(memory=memory, node_time=node_time, target=target, source=source, event_time=event_time, edge_feat=edge_feat, owner_group=owner_group, w_message=w_message, frequency=frequency, phase_shift=phase_shift, w_input=w_input, w_hidden=w_hidden, bias_input=bias_input, bias_hidden=bias_hidden)


def gru_block(pieces, w_input, w_hidden, bias_input, bias_hidden):
    current, averaged, counts = pieces
    mem_width = current.shape[1]
    input_gates = jnp.dot(averaged, w_input, preferred_element_type=jnp.float32) + bias_input
    hidden_gates = jnp.dot(current, w_hidden, preferred_element_type=jnp.float32) + bias_hidden
    reset_gate = jax.nn.sigmoid(input_gates[:, :mem_width] + hidden_gates[:, :mem_width])
    update_gate = jax.nn.sigmoid(input_gates[:, mem_width:2 * mem_width] + hidden_gates[:, mem_width:2 * mem_width])
    candidate = jnp.tanh(input_gates[:, 2 * mem_width:] + reset_gate * hidden_gates[:, 2 * mem_width:])
    previous = current.astype(jnp.float32)
    fresh = (1.0 - update_gate) * candidate + update_gate * previous
    return jnp.where(counts[:, None] > 0, fresh, previous).astype(jnp.bfloat16)


def reference(memory, node_time, target, source, event_time, edge_feat, owner_group, w_message, frequency, phase_shift, w_input, w_hidden, bias_input, bias_hidden):
    mem_width = memory.shape[1]
    time_width = frequency.shape[0]
    group_nodes = N_ROW * NODE_DEV
    node_count = memory.shape[0]
    device_count = node_count // NODE_DEV
    device_of = jnp.arange(target.shape[1], dtype=jnp.int32) // EV_DEV
    group_of = device_of // N_ROW
    current = memory
    times = node_time
    for batch_index in range(B):
        target_now = target[batch_index]
        source_now = source[batch_index]
        valid = target_now >= 0
        target_node = jnp.where(valid, device_of * NODE_DEV + target_now, node_count).astype(jnp.int32)
        source_node = jnp.where(source_now < group_nodes, group_of * group_nodes + source_now,
                                owner_group[batch_index] * group_nodes + source_now - group_nodes).astype(jnp.int32)
        padded_mem = jnp.concatenate([current, jnp.zeros((1, mem_width), jnp.bfloat16)], axis=0)
        padded_time = jnp.concatenate([times, jnp.zeros((1,), jnp.int32)], axis=0)
        mem_target = padded_mem[target_node]
        mem_source = current[source_node]
        last_seen = padded_time[target_node]
        elapsed = (event_time[batch_index] - last_seen).astype(jnp.float32)
        encoded = jnp.cos(elapsed[:, None] * frequency[None, :] + phase_shift[None, :]).astype(jnp.bfloat16)
        base = 2 * mem_width
        message = (jnp.dot(mem_target, w_message[:mem_width], preferred_element_type=jnp.float32)
                   + jnp.dot(mem_source, w_message[mem_width:base], preferred_element_type=jnp.float32)
                   + jnp.dot(encoded, w_message[base:base + time_width], preferred_element_type=jnp.float32)
                   + jnp.dot(edge_feat[batch_index], w_message[base + time_width:], preferred_element_type=jnp.float32)).astype(jnp.bfloat16)
        summed = jax.ops.segment_sum(message.astype(jnp.float32), target_node, node_count + 1)[:node_count]
        counts = jax.ops.segment_sum(valid.astype(jnp.float32), target_node, node_count + 1)[:node_count]
        averaged = (summed / jnp.maximum(counts, 1.0)[:, None]).astype(jnp.bfloat16)
        pieces = (current.reshape(device_count, NODE_DEV, mem_width),
                  averaged.reshape(device_count, NODE_DEV, mem_width),
                  counts.reshape(device_count, NODE_DEV))
        updated = lax.map(lambda piece: gru_block(piece, w_input, w_hidden, bias_input, bias_hidden), pieces)
        current = updated.reshape(node_count, mem_width)
        latest = jax.ops.segment_max(jnp.where(valid, event_time[batch_index], 0).astype(jnp.int32), target_node, node_count + 1)[:node_count]
        times = jnp.maximum(times, latest).astype(jnp.int32)
    return current
```

```python
import functools

import jax
import jax.numpy as jnp
from jax import lax
from jax.experimental import pallas as pl
from jax.experimental.pallas import tpu as pltpu
from jax.sharding import PartitionSpec as P

MESH = pl.DeviceIdType.MESH
LANES = 128
BF = jnp.bfloat16
F32 = jnp.float32
I32 = jnp.int32


def iota(shape, dim):
    return lax.broadcasted_iota(I32, shape, dim)


def onehot(mask):
    return jnp.where(mask, 1.0, 0.0).astype(BF)


def dot(a, b):
    return jnp.dot(a, b, preferred_element_type=F32)


def kernel(
    cfg,
    mem_ref,
    nt_ref,
    tgt_ref,
    src_ref,
    et_ref,
    edge_ref,
    owner_ref,
    wm_ref,
    freq_ref,
    phase_ref,
    wi_ref,
    wh_ref,
    bi_ref,
    bh_ref,
    out_ref,
    ids_send,
    ids_recv,
    colid,
    gmat,
    send,
    recv,
    domr,
    fars,
    place,
    tmat,
    smat,
    touched,
    pmat,
    emat,
    cnt,
    mt,
    part,
    gh,
    msg,
    fresh,
    sems,
):
    doms, rows, nodes, events, width, batches, cap, ocap, ready = cfg
    me_d = lax.axis_index("dom")
    me_r = lax.axis_index("row")
    group_nodes = rows * nodes
    node_bits = nodes.bit_length() - 1
    own_rows = rows * cap
    far_rows = rows * ocap
    IDS_S, IDS_R, IDD_S, IDD_R = range(4)
    OWN_S, OWN_R, DOM_S, DOM_R, FAR_S, FAR_R = (4 + batches * i for i in range(6))

    def row_peer(k):
        return (me_d, lax.rem(me_r + k, rows))

    def dom_peer(q):
        return (lax.rem(me_d + q, doms), me_r)

    def push(src, dst, s, r, peer):
        pltpu.make_async_remote_copy(
            src_ref=src,
            dst_ref=dst,
            send_sem=sems.at[s],
            recv_sem=sems.at[r],
            device_id=peer,
            device_id_type=MESH,
        ).start()

    def drain(ref, s):
        pltpu.make_async_copy(ref, ref, sems.at[s]).wait()

    barrier = pltpu.get_barrier_semaphore()
    for k in range(1, rows):
        pl.semaphore_signal(barrier, inc=1, device_id=row_peer(k), device_id_type=MESH)
    for q in range(1, doms):
        pl.semaphore_signal(barrier, inc=1, device_id=dom_peer(q), device_id_type=MESH)

    stacked = jnp.concatenate(
        [tgt_ref[...], src_ref[...], et_ref[...], et_ref[...]], axis=0
    ).astype(F32)
    cols = stacked.T.astype(I32)
    lane_e = iota((events, events), 1)
    sub_e = iota((events, events), 0)
    lane = iota((events, LANES), 1)

    def locate(s):
        far = s >= group_nodes
        local = jnp.where(far, s - group_nodes, s)
        rel = jnp.bitwise_and((local >> node_bits) - me_r + rows, rows - 1)
        return far, local, rel, jnp.where(far, rel + rows, rel)

    acc_hi = jnp.zeros((rows * 8, LANES), F32)
    acc_lo = jnp.zeros((rows * 8, LANES), F32)
    a_row = iota((rows * 8, events), 0)
    for b in range(batches):
        far_c, _, rel_c, key_c = locate(cols[:, batches + b : batches + b + 1])
        _, local_r, rel_r, key_r = locate(src_ref[b : b + 1, :])
        ahead = jnp.logical_and(key_c == key_r, lane_e < sub_e)
        rank = jnp.sum(jnp.where(ahead, 1.0, 0.0), axis=1, keepdims=True).astype(I32)
        slot = jnp.where(far_c, rank + cap, rank)
        place[b] = jnp.where(far_c, own_rows + rel_c * ocap + rank, rel_c * cap + rank)
        marks = onehot(slot == lane)
        off = jnp.bitwise_and(local_r, nodes - 1) + 1
        mine = jnp.logical_and((a_row >> 3) == rel_r, jnp.bitwise_and(a_row, 7) == b)
        hi = jnp.where(mine, (off >> 8).astype(F32), 0.0).astype(BF)
        lo = jnp.where(mine, jnp.bitwise_and(off, 255).astype(F32), 0.0).astype(BF)
        acc_hi += dot(hi, marks)
        acc_lo += dot(lo, marks)
    ids_send[...] = (acc_hi * 256.0 + acc_lo).astype(I32) - 1
    ids_recv[0, 0:8, :] = ids_send[0:8, :]

    pl.semaphore_wait(barrier, rows - 1 + doms - 1)
    for k in range(1, rows):
        j = rows - k
        push(
            ids_send.at[pl.ds(k * 8, 8)],
            ids_recv.at[0, pl.ds(j * 8, 8)],
            IDS_S,
            IDS_R,
            row_peer(k),
        )
    drain(ids_recv.at[0, pl.ds(8, rows * 8 - 8)], IDS_R)
    for q in range(1, doms):
        push(ids_recv.at[0], ids_recv.at[doms - q], IDD_S, IDD_R, dom_peer(q))

    def spread(q):
        turned = ids_recv[q].astype(F32).T.astype(I32)
        for b in range(batches):
            for k in range(rows):
                col = turned[:, k * 8 + b : k * 8 + b + 1]
                if q == 0:
                    colid[b, k * cap : (k + 1) * cap, :] = jnp.broadcast_to(
                        col[:cap], (cap, LANES)
                    )
                at = own_rows + q * far_rows + k * ocap
                colid[b, at : at + ocap, :] = jnp.broadcast_to(
                    col[cap : cap + ocap], (ocap, LANES)
                )

    def build(b, start, count, to):
        step = LANES
        lanes = iota((step, LANES), 1)

        @pl.loop(0, count // step)
        def _(i):
            c = colid[b, pl.ds(pl.multiple_of(start + i * step, step), step), :]
            for j in range(nodes // LANES):
                gmat[
                    pl.ds(pl.multiple_of(to + i * step, step), step),
                    j * LANES : (j + 1) * LANES,
                ] = onehot(c == lanes + j * LANES)

    def gather(b, table, start, count):
        if ready:
            at = start
        else:
            at = 0
            build(b, start, count, 0)
        found = dot(gmat[at : at + count, :], table[...]).astype(BF)
        send[b, start : start + count, :] = found

    spread(0)
    if ready:
        build(0, 0, own_rows + far_rows, 0)
    if doms > 1:
        drain(ids_recv.at[pl.ds(1, doms - 1)], IDD_R)
    for q in range(1, doms):
        spread(q)
    if ready and doms > 1:
        build(0, own_rows + far_rows, (doms - 1) * far_rows, own_rows + far_rows)

    half = own_rows // 2
    for b in range(batches):
        table = mem_ref if b == 0 else out_ref
        for q in range(1, doms):
            at = own_rows + q * far_rows
            gather(b, table, at, far_rows)
            push(
                send.at[b, pl.ds(at, far_rows)],
                domr.at[b, doms - q - 1],
                DOM_S + b,
                DOM_R + b,
                dom_peer(q),
            )
        for h in range(2):
            gather(b, table, h * half, half)
            if h == 0:
                recv[b, 0:cap, :] = send[b, 0:cap, :]
            for k in range(max(1, h * rows // 2), (h + 1) * rows // 2):
                push(
                    send.at[b, pl.ds(k * cap, cap)],
                    recv.at[b, pl.ds((rows - k) * cap, cap)],
                    OWN_S + b,
                    OWN_R + b,
                    row_peer(k),
                )
        gather(b, table, own_rows, far_rows)

        t_col = cols[:, b : b + 1]
        t_row = tgt_ref[b : b + 1, :]
        t_wide = jnp.broadcast_to(t_col, (events, LANES))
        for j in range(nodes // LANES):
            tmat[:, j * LANES : (j + 1) * LANES] = onehot(t_wide == lane + j * LANES)
        mt[...] = dot(tmat[...], table[...]).astype(BF)

        owner = owner_ref[b : b + 1, :]
        if doms > 1:
            drain(domr.at[b], DOM_R + b)
        picked = send[b, own_rows : own_rows + far_rows, :].astype(F32)
        for q in range(1, doms):
            picked = jnp.where(
                owner == lax.rem(me_d + q, doms), domr[b, q - 1].astype(F32), picked
            )
        fars[b] = picked.astype(BF)
        for k in range(1, rows):
            push(
                fars.at[b, pl.ds(k * ocap, ocap)],
                recv.at[b, pl.ds(own_rows + (rows - k) * ocap, ocap)],
                FAR_S + b,
                FAR_R + b,
                row_peer(k),
            )
        recv[b, own_rows : own_rows + ocap, :] = fars[b, 0:ocap, :]

        same = jnp.logical_and(t_col == t_row, t_col >= 0)
        same_f = jnp.where(same, 1.0, 0.0)
        emat[...] = same_f.astype(BF)
        cnt[...] = jnp.maximum(jnp.sum(same_f, axis=1, keepdims=True), 1.0)
        before = jnp.sum(
            jnp.where(sub_e < lane_e, same_f, 0.0), axis=0, keepdims=True
        )
        s_row = jnp.where(before > 0.0, -1, t_row)

        @pl.loop(0, nodes // 256)
        def _(i):
            at = pl.multiple_of(i * 256, 256)
            hit = jnp.where(iota((256, events), 0) + at == s_row, 1.0, 0.0)
            smat[pl.ds(at, 256), :] = hit.astype(BF)
            touched[pl.ds(at, 256), :] = jnp.sum(hit, axis=1, keepdims=True)

        hi_part = dot(onehot((t_col >> 7) == iota((events, nodes // LANES), 1)), nt_ref[0])
        lo_part = dot(onehot((t_col >> 7) == iota((events, nodes // LANES), 1)), nt_ref[1])
        hit = jnp.bitwise_and(t_col, LANES - 1) == lane
        seen = jnp.sum(
            jnp.where(hit, hi_part * 256.0 + lo_part, 0.0), axis=1, keepdims=True
        )
        for p in range(b):
            times = jnp.where(
                t_col == tgt_ref[p : p + 1, :], et_ref[p : p + 1, :].astype(F32), 0.0
            )
            seen = jnp.maximum(seen, jnp.max(times, axis=1, keepdims=True))
        seen = jnp.where(t_col >= 0, seen, 0.0)
        elapsed = cols[:, 2 * batches + b : 2 * batches + b + 1].astype(F32) - seen
        encoded = jnp.cos(elapsed * freq_ref[...] + phase_ref[...]).astype(BF)
        tw = freq_ref.shape[1]
        part[...] = (
            dot(mt[...], wm_ref[:width, :])
            + dot(encoded, wm_ref[2 * width : 2 * width + tw, :])
            + dot(edge_ref[b], wm_ref[2 * width + tw :, :])
        )
        gh[...] = dot(mt[...], wh_ref[...]) + bh_ref[...]
        for j in range((own_rows + far_rows) // LANES):
            pmat[:, j * LANES : (j + 1) * LANES] = onehot(place[b] == lane + j * LANES)
        if ready and b + 1 < batches:
            build(b + 1, 0, own_rows + doms * far_rows, 0)

        drain(recv.at[b, pl.ds(cap, own_rows - cap)], OWN_R + b)
        drain(recv.at[b, pl.ds(own_rows + ocap, far_rows - ocap)], FAR_R + b)
        ms = dot(pmat[...], recv[b]).astype(BF)
        msg[...] = (part[...] + dot(ms, wm_ref[width : 2 * width, :])).astype(BF)

        @pl.loop(0, events // 128)
        def _(i):
            at = pl.ds(pl.multiple_of(i * 128, 128), 128)
            avg = (dot(emat[at, :], msg[...]) / cnt[at, :]).astype(BF)
            gi = dot(avg, wi_ref[...]) + bi_ref[...]
            g = gh[at, :]
            reset = jax.nn.sigmoid(gi[:, :width] + g[:, :width])
            update = jax.nn.sigmoid(
                gi[:, width : 2 * width] + g[:, width : 2 * width]
            )
            cand = jnp.tanh(gi[:, 2 * width :] + reset * g[:, 2 * width :])
            prev = mt[at, :].astype(F32)
            fresh[at, :] = ((1.0 - update) * cand + update * prev).astype(BF)

        @pl.loop(0, nodes // 512)
        def _(i):
            at = pl.ds(pl.multiple_of(i * 512, 512), 512)
            new = dot(smat[at, :], fresh[...])
            out_ref[at, :] = jnp.where(
                touched[at, :] > 0.0, new, table[at, :].astype(F32)
            ).astype(BF)

    drain(ids_send.at[pl.ds(8, rows * 8 - 8)], IDS_S)
    if doms > 1:
        drain(ids_recv.at[pl.ds(1, doms - 1)], IDD_S)
    for b in range(batches):
        drain(send.at[b, pl.ds(cap, own_rows - cap)], OWN_S + b)
        drain(fars.at[b, pl.ds(ocap, far_rows - ocap)], FAR_S + b)
        if doms > 1:
            drain(domr.at[b], DOM_S + b)


def shards(
    memory,
    node_time,
    target,
    source,
    event_time,
    edge_feat,
    owner_group,
    w_message,
    frequency,
    phase_shift,
    w_input,
    w_hidden,
    bias_input,
    bias_hidden,
):
    nodes, width = memory.shape
    batches, events = target.shape
    rows = lax.axis_size("row")
    doms = lax.axis_size("dom")
    cap = -(-(3 * events // (2 * rows)) // 16) * 16
    ocap = -(-(events // (2 * rows)) // 16) * 16
    slots = rows * (cap + ocap)
    total = rows * cap + doms * rows * ocap
    ready = total <= 2048
    gates = w_input.shape[1]
    nt = node_time.reshape(nodes // LANES, LANES)
    nt = jnp.stack([nt >> 8, nt & 255]).astype(BF)
    owner = jnp.broadcast_to(owner_group[:, None], (batches, width))
    cfg = (doms, rows, nodes, events, width, batches, cap, ocap, ready)
    vm = pltpu.VMEM
    return pl.pallas_call(
        functools.partial(kernel, cfg),
        out_shape=jax.ShapeDtypeStruct((nodes, width), BF),
        in_specs=[pl.BlockSpec(memory_space=vm)] * 14,
        out_specs=pl.BlockSpec(memory_space=vm),
        scratch_shapes=[
            vm((rows * 8, LANES), I32),
            vm((doms, rows * 8, LANES), I32),
            vm((batches, total, LANES), I32),
            vm((total if ready else max(rows * cap // 2, rows * ocap), nodes), BF),
            vm((batches, total, width), BF),
            vm((batches, slots, width), BF),
            vm((batches, max(doms - 1, 1), rows * ocap, width), BF),
            vm((batches, rows * ocap, width), BF),
            vm((batches, events, 1), I32),
            vm((events, nodes), BF),
            vm((nodes, events), BF),
            vm((nodes, 1), F32),
            vm((events, slots), BF),
            vm((events, events), BF),
            vm((events, 1), F32),
            vm((events, width), BF),
            vm((events, width), F32),
            vm((events, gates), F32),
            vm((events, width), BF),
            vm((events, width), BF),
            pltpu.SemaphoreType.DMA((4 + 6 * batches,)),
        ],
        compiler_params=pltpu.CompilerParams(
            collective_id=0,
            has_side_effects=True,
            vmem_limit_bytes=60 * 1024 * 1024,
        ),
    )(
        memory,
        nt,
        target,
        source,
        event_time,
        edge_feat,
        owner,
        w_message,
        frequency.reshape(1, -1),
        phase_shift.reshape(1, -1),
        w_input,
        w_hidden,
        bias_input.reshape(1, -1),
        bias_hidden.reshape(1, -1),
    )


def solution(mesh):
    in_specs = (
        P(("dom", "row"), None),
        P(("dom", "row")),
        P(None, ("dom", "row")),
        P(None, ("dom", "row")),
        P(None, ("dom", "row")),
        P(None, ("dom", "row"), None),
        P(),
        P(),
        P(),
        P(),
        P(),
        P(),
        P(),
        P(),
    )
    out_specs = P(("dom", "row"), None)
    return jax.shard_map(shards, mesh=mesh, in_specs=in_specs, out_specs=out_specs, check_vma=False)
```

```python
import functools

import jax
import jax.numpy as jnp
from jax import lax
from jax.experimental import pallas as pl
from jax.experimental.pallas import tpu as pltpu
from jax.sharding import PartitionSpec as P

MESH = pl.DeviceIdType.MESH
LANES = 128
BF = jnp.bfloat16
F32 = jnp.float32
I32 = jnp.int32


def iota(shape, dim):
    return lax.broadcasted_iota(I32, shape, dim)


def onehot(mask):
    return jnp.where(mask, 1.0, 0.0).astype(BF)


def dot(a, b):
    return jnp.dot(a, b, preferred_element_type=F32)


def kernel(
    cfg,
    mem_ref,
    nt_ref,
    tgt_ref,
    src_ref,
    et_ref,
    edge_ref,
    owner_ref,
    wm_ref,
    freq_ref,
    phase_ref,
    wi_ref,
    wh_ref,
    bi_ref,
    bh_ref,
    out_ref,
    ids_send,
    ids_recv,
    colid,
    gmat,
    send,
    recv,
    domr,
    fars,
    place,
    tmat,
    smat,
    touched,
    pmat,
    emat,
    cnt,
    mt,
    part,
    gh,
    gi,
    fresh,
    qmat,
    hits,
    turned,
    sems,
):
    doms, rows, nodes, events, width, batches, cap, ocap, ready = cfg
    me_d = lax.axis_index("dom")
    me_r = lax.axis_index("row")
    group_nodes = rows * nodes
    node_bits = nodes.bit_length() - 1
    own_rows = rows * cap
    far_rows = rows * ocap
    total = own_rows + doms * far_rows
    IDS_S, IDS_R, IDD_S, IDD_R = range(4)
    OWN_S, OWN_R, DOM_S, DOM_R, FAR_S, FAR_R = (4 + batches * i for i in range(6))

    def row_peer(k):
        return (me_d, lax.rem(me_r + k, rows))

    def dom_peer(q):
        return (lax.rem(me_d + q, doms), me_r)

    def push(src, dst, s, r, peer):
        pltpu.make_async_remote_copy(
            src_ref=src,
            dst_ref=dst,
            send_sem=sems.at[s],
            recv_sem=sems.at[r],
            device_id=peer,
            device_id_type=MESH,
        ).start()

    def drain(ref, s):
        pltpu.make_async_copy(ref, ref, sems.at[s]).wait()

    barrier = pltpu.get_barrier_semaphore()
    for k in range(1, rows):
        pl.semaphore_signal(barrier, inc=1, device_id=row_peer(k), device_id_type=MESH)
    for q in range(1, doms):
        pl.semaphore_signal(barrier, inc=1, device_id=dom_peer(q), device_id_type=MESH)

    stacked = jnp.concatenate(
        [tgt_ref[...], src_ref[...], et_ref[...], et_ref[...]], axis=0
    ).astype(F32)
    cols = stacked.T.astype(I32)
    lane_e = iota((events, events), 1)
    sub_e = iota((events, events), 0)
    lane = iota((events, LANES), 1)

    def locate(s):
        far = s >= group_nodes
        local = jnp.where(far, s - group_nodes, s)
        rel = jnp.bitwise_and((local >> node_bits) - me_r + rows, rows - 1)
        return far, local, rel, jnp.where(far, rel + rows, rel)

    acc_hi = jnp.zeros((rows * 8, LANES), F32)
    acc_lo = jnp.zeros((rows * 8, LANES), F32)
    a_row = iota((rows * 8, events), 0)
    for b in range(batches):
        far_c, _, rel_c, key_c = locate(cols[:, batches + b : batches + b + 1])
        _, local_r, rel_r, key_r = locate(src_ref[b : b + 1, :])
        ahead = jnp.logical_and(key_c == key_r, lane_e < sub_e)
        rank = jnp.sum(jnp.where(ahead, 1.0, 0.0), axis=1, keepdims=True).astype(I32)
        slot = jnp.where(far_c, rank + cap, rank)
        place[b] = jnp.where(far_c, own_rows + rel_c * ocap + rank, rel_c * cap + rank)
        marks = onehot(slot == lane)
        off = jnp.bitwise_and(local_r, nodes - 1) + 1
        mine = jnp.logical_and((a_row >> 3) == rel_r, jnp.bitwise_and(a_row, 7) == b)
        hi = jnp.where(mine, (off >> 8).astype(F32), 0.0).astype(BF)
        lo = jnp.where(mine, jnp.bitwise_and(off, 255).astype(F32), 0.0).astype(BF)
        acc_hi += dot(hi, marks)
        acc_lo += dot(lo, marks)
    ids_send[...] = (acc_hi * 256.0 + acc_lo).astype(I32) - 1
    ids_recv[0, 0:8, :] = ids_send[0:8, :]

    pl.semaphore_wait(barrier, rows - 1 + doms - 1)
    for k in range(1, rows):
        j = rows - k
        push(
            ids_send.at[pl.ds(k * 8, 8)],
            ids_recv.at[0, pl.ds(j * 8, 8)],
            IDS_S,
            IDS_R,
            row_peer(k),
        )
    drain(ids_recv.at[0, pl.ds(8, rows * 8 - 8)], IDS_R)
    for q in range(1, doms):
        push(ids_recv.at[0], ids_recv.at[doms - q], IDD_S, IDD_R, dom_peer(q))

    def spread(q, b):
        for k in range(rows):
            col = turned[q, :, k * 8 + b : k * 8 + b + 1]
            if q == 0:
                colid[k * cap : (k + 1) * cap, :] = jnp.broadcast_to(
                    col[:cap], (cap, LANES)
                )
            at = own_rows + q * far_rows + k * ocap
            colid[at : at + ocap, :] = jnp.broadcast_to(
                col[cap : cap + ocap], (ocap, LANES)
            )

    def build(start, count, to):
        step = 64
        lanes = iota((step, LANES), 1)

        @pl.loop(0, count // step)
        def _(i):
            c = colid[pl.ds(pl.multiple_of(start + i * step, step), step), :]
            for j in range(nodes // LANES):
                gmat[
                    pl.ds(pl.multiple_of(to + i * step, step), step),
                    j * LANES : (j + 1) * LANES,
                ] = onehot(c == lanes + j * LANES)

    def gather(b, table, start, count):
        if ready:
            at = start
        else:
            at = 0
            build(start, count, 0)
        found = dot(gmat[at : at + count, :], table[...]).astype(BF)
        send[b, start : start + count, :] = found

    def link(s_row):
        step = 64

        @pl.loop(0, total // step)
        def _(i):
            at = pl.ds(pl.multiple_of(i * step, step), step)
            c = colid[at, :]
            met = jnp.zeros((step, LANES), F32)
            for j in range(events // LANES):
                hit = jnp.where(c == s_row[:, j * LANES : (j + 1) * LANES], 1.0, 0.0)
                qmat[at, j * LANES : (j + 1) * LANES] = hit.astype(BF)
                met += hit
            hits[at, :] = jnp.sum(met, axis=1, keepdims=True)

    def renew(b, start, count):
        at = slice(start, start + count)
        send[b, at, :] = jnp.where(
            hits[at, :] > 0.0, dot(qmat[at, :], fresh[...]), send[b, at, :].astype(F32)
        ).astype(BF)

    def settle(old):
        @pl.loop(0, nodes // 512)
        def _(i):
            at = pl.ds(pl.multiple_of(i * 512, 512), 512)
            new = dot(smat[at, :], fresh[...])
            out_ref[at, :] = jnp.where(
                touched[at, :] > 0.0, new, old[at, :].astype(F32)
            ).astype(BF)

    def row_of(ref):
        return jnp.concatenate(
            [ref[i : i + 1, :] for i in range(ref.shape[0])], axis=1
        )

    bias_i = row_of(bi_ref)
    bias_h = row_of(bh_ref)
    bias_wide = bias_h + jnp.where(
        iota(bias_i.shape, 1) < 2 * width, bias_i, jnp.zeros_like(bias_i)
    )

    turned[0] = ids_recv[0].astype(F32).T.astype(I32)
    spread(0, 0)
    if ready:
        build(0, own_rows + far_rows, 0)
    if doms > 1:
        drain(ids_recv.at[pl.ds(1, doms - 1)], IDD_R)
    for q in range(1, doms):
        turned[q] = ids_recv[q].astype(F32).T.astype(I32)
        spread(q, 0)
    if ready and doms > 1:
        build(own_rows + far_rows, (doms - 1) * far_rows, own_rows + far_rows)

    quarter = rows // 4
    parts = (
        (quarter, 3 * quarter),
        (0, quarter),
        (3 * quarter, rows),
    )
    for b in range(batches):
        table = mem_ref if b == 0 else out_ref

        def supply(start, count):
            if b == 0:
                gather(0, table, start, count)
            else:
                renew(b, start, count)

        for q in range(1, doms):
            at = own_rows + q * far_rows
            supply(at, far_rows)
            push(
                send.at[b, pl.ds(at, far_rows)],
                domr.at[b, doms - q - 1],
                DOM_S + b,
                DOM_R + b,
                dom_peer(q),
            )
        for first, last in parts:
            supply(first * cap, (last - first) * cap)
            for k in sorted(range(max(1, first), last), key=lambda k: abs(2 * k - rows)):
                push(
                    send.at[b, pl.ds(k * cap, cap)],
                    recv.at[b, pl.ds((rows - k) * cap, cap)],
                    OWN_S + b,
                    OWN_R + b,
                    row_peer(k),
                )
        supply(own_rows, far_rows)
        recv[b, 0:cap, :] = send[b, 0:cap, :]
        if b > 0:
            settle(mem_ref if b == 1 else out_ref)

        t_col = cols[:, b : b + 1]
        t_row = tgt_ref[b : b + 1, :]
        t_wide = jnp.broadcast_to(t_col, (events, LANES))
        for j in range(nodes // LANES):
            tmat[:, j * LANES : (j + 1) * LANES] = onehot(t_wide == lane + j * LANES)
        mt[...] = dot(tmat[...], table[...]).astype(BF)

        owner = jnp.full((1, width), owner_ref[b], I32)
        if doms > 1:
            drain(domr.at[b], DOM_R + b)
        picked = send[b, own_rows : own_rows + far_rows, :].astype(F32)
        for q in range(1, doms):
            picked = jnp.where(
                owner == lax.rem(me_d + q, doms), domr[b, q - 1].astype(F32), picked
            )
        fars[b] = picked.astype(BF)
        for k in sorted(range(1, rows), key=lambda k: abs(2 * k - rows)):
            push(
                fars.at[b, pl.ds(k * ocap, ocap)],
                recv.at[b, pl.ds(own_rows + (rows - k) * ocap, ocap)],
                FAR_S + b,
                FAR_R + b,
                row_peer(k),
            )
        recv[b, own_rows : own_rows + ocap, :] = fars[b, 0:ocap, :]

        same = jnp.logical_and(t_col == t_row, t_col >= 0)
        same_f = jnp.where(same, 1.0, 0.0)
        emat[...] = same_f.astype(BF)
        cnt[...] = 1.0 / jnp.maximum(jnp.sum(same_f, axis=1, keepdims=True), 1.0)
        before = jnp.sum(
            jnp.where(sub_e < lane_e, same_f, 0.0), axis=0, keepdims=True
        )
        s_row = jnp.where(jnp.logical_or(before > 0.0, t_row < 0), -2, t_row)

        @pl.loop(0, nodes // 256)
        def _(i):
            at = pl.multiple_of(i * 256, 256)
            hit = jnp.where(iota((256, events), 0) + at == s_row, 1.0, 0.0)
            smat[pl.ds(at, 256), :] = hit.astype(BF)
            touched[pl.ds(at, 256), :] = jnp.sum(hit, axis=1, keepdims=True)

        block = onehot((t_col >> 7) == iota((events, nodes // LANES), 1))
        hi_part = dot(block, (nt_ref[...] >> 8).astype(F32).astype(BF))
        lo_part = dot(block, jnp.bitwise_and(nt_ref[...], 255).astype(F32).astype(BF))
        hit = jnp.bitwise_and(t_col, LANES - 1) == lane
        seen = jnp.sum(
            jnp.where(hit, hi_part * 256.0 + lo_part, 0.0), axis=1, keepdims=True
        )
        for p in range(b):
            times = jnp.where(
                t_col == tgt_ref[p : p + 1, :], et_ref[p : p + 1, :].astype(F32), 0.0
            )
            seen = jnp.maximum(seen, jnp.max(times, axis=1, keepdims=True))
        seen = jnp.where(t_col >= 0, seen, 0.0)
        elapsed = cols[:, 2 * batches + b : 2 * batches + b + 1].astype(F32) - seen
        encoded = jnp.cos(elapsed * freq_ref[...] + phase_ref[...]).astype(BF)
        tw = freq_ref.shape[1]
        part[...] = (
            dot(mt[...], wm_ref[:width, :])
            + dot(encoded, wm_ref[2 * width : 2 * width + tw, :])
            + dot(edge_ref[b], wm_ref[2 * width + tw :, :])
        )
        gh[...] = dot(mt[...], wh_ref[...]) + bias_wide
        for j in range((own_rows + far_rows) // LANES):
            pmat[:, j * LANES : (j + 1) * LANES] = onehot(place[b] == lane + j * LANES)
        if b + 1 < batches:
            for q in range(doms):
                spread(q, b + 1)
            if ready:
                build(0, total, 0)
            for start, count in (
                (0, own_rows // 2),
                (own_rows // 2, own_rows // 2),
                *((own_rows + q * far_rows, far_rows) for q in range(doms)),
            ):
                gather(b + 1, table, start, count)
            link(s_row)

        drain(recv.at[b, pl.ds(cap, own_rows - cap)], OWN_R + b)
        near = dot(pmat[:, :own_rows], recv[b, :own_rows, :])
        drain(recv.at[b, pl.ds(own_rows + ocap, far_rows - ocap)], FAR_R + b)
        ms = (near + dot(pmat[:, own_rows:], recv[b, own_rows:, :])).astype(BF)
        msg = (part[...] + dot(ms, wm_ref[width : 2 * width, :])).astype(BF)
        avg = (dot(emat[...], msg) * cnt[...]).astype(BF)
        gi[...] = dot(avg, wi_ref[...])

        for i in range(events // 64):
            at = slice(i * 64, (i + 1) * 64)
            g = gh[at, :]
            gates = 0.5 * jnp.tanh(0.5 * (gi[at, : 2 * width] + g[:, : 2 * width])) + 0.5
            reset = gates[:, :width]
            update = gates[:, width:]
            cand = jnp.tanh(
                gi[at, 2 * width :] + bias_i[:, 2 * width :] + reset * g[:, 2 * width :]
            )
            prev = mt[at, :].astype(F32)
            fresh[at, :] = ((1.0 - update) * cand + update * prev).astype(BF)

    settle(out_ref if batches > 1 else mem_ref)
    drain(ids_send.at[pl.ds(8, rows * 8 - 8)], IDS_S)
    if doms > 1:
        drain(ids_recv.at[pl.ds(1, doms - 1)], IDD_S)
    for b in range(batches):
        drain(send.at[b, pl.ds(cap, own_rows - cap)], OWN_S + b)
        drain(fars.at[b, pl.ds(ocap, far_rows - ocap)], FAR_S + b)
        if doms > 1:
            drain(domr.at[b], DOM_S + b)


def shards(
    memory,
    node_time,
    target,
    source,
    event_time,
    edge_feat,
    owner_group,
    w_message,
    frequency,
    phase_shift,
    w_input,
    w_hidden,
    bias_input,
    bias_hidden,
):
    nodes, width = memory.shape
    batches, events = target.shape
    rows = lax.axis_size("row")
    doms = lax.axis_size("dom")
    cap = -(-(3 * events // (2 * rows)) // 16) * 16
    ocap = -(-(events // (2 * rows)) // 16) * 16
    slots = rows * (cap + ocap)
    total = rows * cap + doms * rows * ocap
    ready = total <= 2048
    gates = w_input.shape[1]
    nt = node_time.reshape(nodes // LANES, LANES)
    cfg = (doms, rows, nodes, events, width, batches, cap, ocap, ready)
    vm = pltpu.VMEM
    return pl.pallas_call(
        functools.partial(kernel, cfg),
        out_shape=jax.ShapeDtypeStruct((nodes, width), BF),
        in_specs=[
            pl.BlockSpec(memory_space=pltpu.SMEM if i == 6 else vm) for i in range(14)
        ],
        out_specs=pl.BlockSpec(memory_space=vm),
        scratch_shapes=[
            vm((rows * 8, LANES), I32),
            vm((doms, rows * 8, LANES), I32),
            vm((total, LANES), I32),
            vm((total if ready else max(rows * cap // 2, rows * ocap), nodes), BF),
            vm((batches, total, width), BF),
            vm((batches, slots, width), BF),
            vm((batches, max(doms - 1, 1), rows * ocap, width), BF),
            vm((batches, rows * ocap, width), BF),
            vm((batches, events, 1), I32),
            vm((events, nodes), BF),
            vm((nodes, events), BF),
            vm((nodes, 1), F32),
            vm((events, slots), BF),
            vm((events, events), BF),
            vm((events, 1), F32),
            vm((events, width), BF),
            vm((events, width), F32),
            vm((events, gates), F32),
            vm((events, gates), F32),
            vm((events, width), BF),
            vm((total, events), BF),
            vm((total, 1), F32),
            vm((doms, LANES, rows * 8), I32),
            pltpu.SemaphoreType.DMA((4 + 6 * batches,)),
        ],
        compiler_params=pltpu.CompilerParams(
            collective_id=0,
            has_side_effects=True,
            vmem_limit_bytes=60 * 1024 * 1024,
        ),
    )(
        memory,
        nt,
        target,
        source,
        event_time,
        edge_feat,
        owner_group,
        w_message,
        frequency.reshape(1, -1),
        phase_shift.reshape(1, -1),
        w_input,
        w_hidden,
        bias_input.reshape(-1, LANES),
        bias_hidden.reshape(-1, LANES),
    )


def solution(mesh):
    in_specs = (
        P(("dom", "row"), None),
        P(("dom", "row")),
        P(None, ("dom", "row")),
        P(None, ("dom", "row")),
        P(None, ("dom", "row")),
        P(None, ("dom", "row"), None),
        P(),
        P(),
        P(),
        P(),
        P(),
        P(),
        P(),
        P(),
    )
    out_specs = P(("dom", "row"), None)
    return jax.shard_map(shards, mesh=mesh, in_specs=in_specs, out_specs=out_specs, check_vma=False)
```

```python
import functools

import jax
import jax.numpy as jnp
from jax import lax
from jax.experimental import pallas as pl
from jax.experimental.pallas import tpu as pltpu
from jax.sharding import PartitionSpec as P

MESH = pl.DeviceIdType.MESH
LANES = 128
BF = jnp.bfloat16
F32 = jnp.float32
I32 = jnp.int32


def iota(shape, dim):
    return lax.broadcasted_iota(I32, shape, dim)


def onehot(mask):
    return jnp.where(mask, 1.0, 0.0).astype(BF)


def dot(a, b):
    return jnp.dot(a, b, preferred_element_type=F32)


def kernel(
    cfg,
    mem_ref,
    nt_ref,
    tgt_ref,
    src_ref,
    et_ref,
    edge_ref,
    owner_ref,
    wm_ref,
    freq_ref,
    phase_ref,
    wi_ref,
    wh_ref,
    bi_ref,
    bh_ref,
    out_ref,
    ids_send,
    ids_recv,
    colid,
    gmat,
    send,
    recv,
    domr,
    fars,
    place,
    tmat,
    smat,
    touched,
    pmat,
    emat,
    cnt,
    mt,
    part,
    gh,
    gi,
    fresh,
    qmat,
    hits,
    turned,
    sems,
):
    doms, rows, nodes, events, width, batches, cap, ocap, ready = cfg
    me_d = lax.axis_index("dom")
    me_r = lax.axis_index("row")
    group_nodes = rows * nodes
    node_bits = nodes.bit_length() - 1
    own_rows = rows * cap
    far_rows = rows * ocap
    total = own_rows + doms * far_rows
    IDS_S, IDS_R, IDD_S, IDD_R = range(4)
    OWN_S, OWN_R, DOM_S, DOM_R, FAR_S, FAR_R = (4 + batches * i for i in range(6))

    def row_peer(k):
        return (me_d, lax.rem(me_r + k, rows))

    def dom_peer(q):
        return (lax.rem(me_d + q, doms), me_r)

    def push(src, dst, s, r, peer):
        pltpu.make_async_remote_copy(
            src_ref=src,
            dst_ref=dst,
            send_sem=sems.at[s],
            recv_sem=sems.at[r],
            device_id=peer,
            device_id_type=MESH,
        ).start()

    def drain(ref, s):
        pltpu.make_async_copy(ref, ref, sems.at[s]).wait()

    barrier = pltpu.get_barrier_semaphore()
    for k in range(1, rows):
        pl.semaphore_signal(barrier, inc=1, device_id=row_peer(k), device_id_type=MESH)
    for q in range(1, doms):
        pl.semaphore_signal(barrier, inc=1, device_id=dom_peer(q), device_id_type=MESH)

    stacked = jnp.concatenate(
        [tgt_ref[...], src_ref[...], et_ref[...], et_ref[...]], axis=0
    ).astype(F32)
    cols = stacked.T.astype(I32)
    lane_e = iota((events, events), 1)
    sub_e = iota((events, events), 0)
    lane = iota((events, LANES), 1)

    def locate(s):
        far = s >= group_nodes
        local = jnp.where(far, s - group_nodes, s)
        rel = jnp.bitwise_and((local >> node_bits) - me_r + rows, rows - 1)
        return far, local, rel, jnp.where(far, rel + rows, rel)

    acc_hi = jnp.zeros((rows * 8, LANES), F32)
    acc_lo = jnp.zeros((rows * 8, LANES), F32)
    a_row = iota((rows * 8, events), 0)
    for b in range(batches):
        far_c, _, rel_c, key_c = locate(cols[:, batches + b : batches + b + 1])
        _, local_r, rel_r, key_r = locate(src_ref[b : b + 1, :])
        ahead = jnp.logical_and(key_c == key_r, lane_e < sub_e)
        rank = jnp.sum(jnp.where(ahead, 1.0, 0.0), axis=1, keepdims=True).astype(I32)
        slot = jnp.where(far_c, rank + cap, rank)
        place[b] = jnp.where(far_c, own_rows + rel_c * ocap + rank, rel_c * cap + rank)
        marks = onehot(slot == lane)
        off = jnp.bitwise_and(local_r, nodes - 1) + 1
        mine = jnp.logical_and((a_row >> 3) == rel_r, jnp.bitwise_and(a_row, 7) == b)
        hi = jnp.where(mine, (off >> 8).astype(F32), 0.0).astype(BF)
        lo = jnp.where(mine, jnp.bitwise_and(off, 255).astype(F32), 0.0).astype(BF)
        acc_hi += dot(hi, marks)
        acc_lo += dot(lo, marks)
    ids_send[...] = (acc_hi * 256.0 + acc_lo).astype(I32) - 1
    ids_recv[0, 0:8, :] = ids_send[0:8, :]

    pl.semaphore_wait(barrier, rows - 1 + doms - 1)
    for k in range(1, rows):
        j = rows - k
        push(
            ids_send.at[pl.ds(k * 8, 8)],
            ids_recv.at[0, pl.ds(j * 8, 8)],
            IDS_S,
            IDS_R,
            row_peer(k),
        )
    drain(ids_recv.at[0, pl.ds(8, rows * 8 - 8)], IDS_R)
    for q in range(1, doms):
        push(ids_recv.at[0], ids_recv.at[doms - q], IDD_S, IDD_R, dom_peer(q))

    def spread(q, b):
        for k in range(rows):
            col = turned[q, :, k * 8 + b : k * 8 + b + 1]
            if q == 0:
                colid[k * cap : (k + 1) * cap, :] = jnp.broadcast_to(
                    col[:cap], (cap, LANES)
                )
            at = own_rows + q * far_rows + k * ocap
            colid[at : at + ocap, :] = jnp.broadcast_to(
                col[cap : cap + ocap], (ocap, LANES)
            )

    def build(start, count, to):
        step = 64
        lanes = iota((step, LANES), 1)

        @pl.loop(0, count // step)
        def _(i):
            c = colid[pl.ds(pl.multiple_of(start + i * step, step), step), :]
            for j in range(nodes // LANES):
                gmat[
                    pl.ds(pl.multiple_of(to + i * step, step), step),
                    j * LANES : (j + 1) * LANES,
                ] = onehot(c == lanes + j * LANES)

    def gather(b, table, start, count):
        if ready:
            at = start
        else:
            at = 0
            build(start, count, 0)
        found = dot(gmat[at : at + count, :], table[...]).astype(BF)
        send[b, start : start + count, :] = found

    def link(s_row):
        step = 64

        @pl.loop(0, total // step)
        def _(i):
            at = pl.ds(pl.multiple_of(i * step, step), step)
            c = colid[at, :]
            met = jnp.zeros((step, LANES), F32)
            for j in range(events // LANES):
                hit = jnp.where(c == s_row[:, j * LANES : (j + 1) * LANES], 1.0, 0.0)
                qmat[at, j * LANES : (j + 1) * LANES] = hit.astype(BF)
                met += hit
            hits[at, :] = jnp.sum(met, axis=1, keepdims=True)

    def renew(b, start, count):
        at = slice(start, start + count)
        send[b, at, :] = jnp.where(
            hits[at, :] > 0.0, dot(qmat[at, :], fresh[...]), send[b, at, :].astype(F32)
        ).astype(BF)

    def settle(old):
        @pl.loop(0, nodes // 512)
        def _(i):
            at = pl.ds(pl.multiple_of(i * 512, 512), 512)
            new = dot(smat[at, :], fresh[...])
            out_ref[at, :] = jnp.where(
                touched[at, :] > 0.0, new, old[at, :].astype(F32)
            ).astype(BF)

    def row_of(ref):
        return jnp.concatenate(
            [ref[i : i + 1, :] for i in range(ref.shape[0])], axis=1
        )

    bias_i = row_of(bi_ref)
    bias_h = row_of(bh_ref)
    bias_wide = bias_h + jnp.where(
        iota(bias_i.shape, 1) < 2 * width, bias_i, jnp.zeros_like(bias_i)
    )

    turned[0] = ids_recv[0].astype(F32).T.astype(I32)
    spread(0, 0)
    if ready:
        build(0, own_rows, 0)

    def rest_of_ids():
        if doms > 1:
            drain(ids_recv.at[pl.ds(1, doms - 1)], IDD_R)
        for q in range(1, doms):
            turned[q] = ids_recv[q].astype(F32).T.astype(I32)
            spread(q, 0)
        if ready:
            build(own_rows, doms * far_rows, own_rows)

    quarter = rows // 4
    parts = (
        (quarter, 3 * quarter),
        (0, quarter),
        (3 * quarter, rows),
    )
    for b in range(batches):
        table = mem_ref if b == 0 else out_ref

        def supply(start, count):
            if b == 0:
                gather(0, table, start, count)
            else:
                renew(b, start, count)

        def send_dom():
            for q in range(1, doms):
                at = own_rows + q * far_rows
                supply(at, far_rows)
                push(
                    send.at[b, pl.ds(at, far_rows)],
                    domr.at[b, doms - q - 1],
                    DOM_S + b,
                    DOM_R + b,
                    dom_peer(q),
                )

        def send_own():
            for first, last in parts:
                supply(first * cap, (last - first) * cap)
                for k in sorted(range(max(1, first), last), key=lambda k: abs(2 * k - rows)):
                    push(
                        send.at[b, pl.ds(k * cap, cap)],
                        recv.at[b, pl.ds((rows - k) * cap, cap)],
                        OWN_S + b,
                        OWN_R + b,
                        row_peer(k),
                    )

        if b == 0:
            send_own()
            rest_of_ids()
            send_dom()
        else:
            send_dom()
            send_own()
        supply(own_rows, far_rows)
        recv[b, 0:cap, :] = send[b, 0:cap, :]
        if b > 0:
            settle(mem_ref if b == 1 else out_ref)

        t_col = cols[:, b : b + 1]
        t_row = tgt_ref[b : b + 1, :]
        t_wide = jnp.broadcast_to(t_col, (events, LANES))
        for j in range(nodes // LANES):
            tmat[:, j * LANES : (j + 1) * LANES] = onehot(t_wide == lane + j * LANES)
        mt[...] = dot(tmat[...], table[...]).astype(BF)

        owner = jnp.full((1, width), owner_ref[b], I32)
        if doms > 1:
            drain(domr.at[b], DOM_R + b)
        picked = send[b, own_rows : own_rows + far_rows, :].astype(F32)
        for q in range(1, doms):
            picked = jnp.where(
                owner == lax.rem(me_d + q, doms), domr[b, q - 1].astype(F32), picked
            )
        fars[b] = picked.astype(BF)
        for k in sorted(range(1, rows), key=lambda k: abs(2 * k - rows)):
            push(
                fars.at[b, pl.ds(k * ocap, ocap)],
                recv.at[b, pl.ds(own_rows + (rows - k) * ocap, ocap)],
                FAR_S + b,
                FAR_R + b,
                row_peer(k),
            )
        recv[b, own_rows : own_rows + ocap, :] = fars[b, 0:ocap, :]

        same = jnp.logical_and(t_col == t_row, t_col >= 0)
        same_f = jnp.where(same, 1.0, 0.0)
        emat[...] = same_f.astype(BF)
        cnt[...] = 1.0 / jnp.maximum(jnp.sum(same_f, axis=1, keepdims=True), 1.0)
        before = jnp.sum(
            jnp.where(sub_e < lane_e, same_f, 0.0), axis=0, keepdims=True
        )
        s_row = jnp.where(jnp.logical_or(before > 0.0, t_row < 0), -2, t_row)

        @pl.loop(0, nodes // 256)
        def _(i):
            at = pl.multiple_of(i * 256, 256)
            hit = jnp.where(iota((256, events), 0) + at == s_row, 1.0, 0.0)
            smat[pl.ds(at, 256), :] = hit.astype(BF)
            touched[pl.ds(at, 256), :] = jnp.sum(hit, axis=1, keepdims=True)

        block = onehot((t_col >> 7) == iota((events, nodes // LANES), 1))
        hi_part = dot(block, (nt_ref[...] >> 8).astype(F32).astype(BF))
        lo_part = dot(block, jnp.bitwise_and(nt_ref[...], 255).astype(F32).astype(BF))
        hit = jnp.bitwise_and(t_col, LANES - 1) == lane
        seen = jnp.sum(
            jnp.where(hit, hi_part * 256.0 + lo_part, 0.0), axis=1, keepdims=True
        )
        for p in range(b):
            times = jnp.where(
                t_col == tgt_ref[p : p + 1, :], et_ref[p : p + 1, :].astype(F32), 0.0
            )
            seen = jnp.maximum(seen, jnp.max(times, axis=1, keepdims=True))
        seen = jnp.where(t_col >= 0, seen, 0.0)
        elapsed = cols[:, 2 * batches + b : 2 * batches + b + 1].astype(F32) - seen
        encoded = jnp.cos(elapsed * freq_ref[...] + phase_ref[...]).astype(BF)
        tw = freq_ref.shape[1]
        part[...] = (
            dot(mt[...], wm_ref[:width, :])
            + dot(encoded, wm_ref[2 * width : 2 * width + tw, :])
            + dot(edge_ref[b], wm_ref[2 * width + tw :, :])
        )
        gh[...] = dot(mt[...], wh_ref[...]) + bias_wide
        for j in range((own_rows + far_rows) // LANES):
            pmat[:, j * LANES : (j + 1) * LANES] = onehot(place[b] == lane + j * LANES)
        if b + 1 < batches:
            for q in range(doms):
                spread(q, b + 1)
            if ready:
                build(0, total, 0)
            for start, count in (
                (0, own_rows // 2),
                (own_rows // 2, own_rows // 2),
                *((own_rows + q * far_rows, far_rows) for q in range(doms)),
            ):
                gather(b + 1, table, start, count)
            link(s_row)

        drain(recv.at[b, pl.ds(cap, own_rows - cap)], OWN_R + b)
        near = dot(pmat[:, :own_rows], recv[b, :own_rows, :])
        drain(recv.at[b, pl.ds(own_rows + ocap, far_rows - ocap)], FAR_R + b)
        ms = (near + dot(pmat[:, own_rows:], recv[b, own_rows:, :])).astype(BF)
        msg = (part[...] + dot(ms, wm_ref[width : 2 * width, :])).astype(BF)
        avg = (dot(emat[...], msg) * cnt[...]).astype(BF)
        gi[...] = dot(avg, wi_ref[...])

        for i in range(events // 64):
            at = slice(i * 64, (i + 1) * 64)
            g = gh[at, :]
            gates = 0.5 * jnp.tanh(0.5 * (gi[at, : 2 * width] + g[:, : 2 * width])) + 0.5
            reset = gates[:, :width]
            update = gates[:, width:]
            cand = jnp.tanh(
                gi[at, 2 * width :] + bias_i[:, 2 * width :] + reset * g[:, 2 * width :]
            )
            prev = mt[at, :].astype(F32)
            fresh[at, :] = ((1.0 - update) * cand + update * prev).astype(BF)

    settle(out_ref if batches > 1 else mem_ref)
    drain(ids_send.at[pl.ds(8, rows * 8 - 8)], IDS_S)
    if doms > 1:
        drain(ids_recv.at[pl.ds(1, doms - 1)], IDD_S)
    for b in range(batches):
        drain(send.at[b, pl.ds(cap, own_rows - cap)], OWN_S + b)
        drain(fars.at[b, pl.ds(ocap, far_rows - ocap)], FAR_S + b)
        if doms > 1:
            drain(domr.at[b], DOM_S + b)


def shards(
    memory,
    node_time,
    target,
    source,
    event_time,
    edge_feat,
    owner_group,
    w_message,
    frequency,
    phase_shift,
    w_input,
    w_hidden,
    bias_input,
    bias_hidden,
):
    nodes, width = memory.shape
    batches, events = target.shape
    rows = lax.axis_size("row")
    doms = lax.axis_size("dom")
    cap = -(-(3 * events // (2 * rows)) // 16) * 16
    ocap = -(-(events // (2 * rows)) // 16) * 16
    slots = rows * (cap + ocap)
    total = rows * cap + doms * rows * ocap
    ready = total <= 2048
    gates = w_input.shape[1]
    nt = node_time.reshape(nodes // LANES, LANES)
    cfg = (doms, rows, nodes, events, width, batches, cap, ocap, ready)
    vm = pltpu.VMEM
    return pl.pallas_call(
        functools.partial(kernel, cfg),
        out_shape=jax.ShapeDtypeStruct((nodes, width), BF),
        in_specs=[
            pl.BlockSpec(memory_space=pltpu.SMEM if i == 6 else vm) for i in range(14)
        ],
        out_specs=pl.BlockSpec(memory_space=vm),
        scratch_shapes=[
            vm((rows * 8, LANES), I32),
            vm((doms, rows * 8, LANES), I32),
            vm((total, LANES), I32),
            vm((total if ready else max(rows * cap // 2, rows * ocap), nodes), BF),
            vm((batches, total, width), BF),
            vm((batches, slots, width), BF),
            vm((batches, max(doms - 1, 1), rows * ocap, width), BF),
            vm((batches, rows * ocap, width), BF),
            vm((batches, events, 1), I32),
            vm((events, nodes), BF),
            vm((nodes, events), BF),
            vm((nodes, 1), F32),
            vm((events, slots), BF),
            vm((events, events), BF),
            vm((events, 1), F32),
            vm((events, width), BF),
            vm((events, width), F32),
            vm((events, gates), F32),
            vm((events, gates), F32),
            vm((events, width), BF),
            vm((total, events), BF),
            vm((total, 1), F32),
            vm((doms, LANES, rows * 8), I32),
            pltpu.SemaphoreType.DMA((4 + 6 * batches,)),
        ],
        compiler_params=pltpu.CompilerParams(
            collective_id=0,
            has_side_effects=True,
            vmem_limit_bytes=60 * 1024 * 1024,
        ),
    )(
        memory,
        nt,
        target,
        source,
        event_time,
        edge_feat,
        owner_group,
        w_message,
        frequency.reshape(1, -1),
        phase_shift.reshape(1, -1),
        w_input,
        w_hidden,
        bias_input.reshape(-1, LANES),
        bias_hidden.reshape(-1, LANES),
    )


def solution(mesh):
    in_specs = (
        P(("dom", "row"), None),
        P(("dom", "row")),
        P(None, ("dom", "row")),
        P(None, ("dom", "row")),
        P(None, ("dom", "row")),
        P(None, ("dom", "row"), None),
        P(),
        P(),
        P(),
        P(),
        P(),
        P(),
        P(),
        P(),
    )
    out_specs = P(("dom", "row"), None)
    return jax.shard_map(shards, mesh=mesh, in_specs=in_specs, out_specs=out_specs, check_vma=False)
```
